128 devices in a mesh: row: 8 (over y, z_lo), col: 16 (over x, z_hi, core).
Axes of the slice: x: 4, y: 4, z: 4 (z_hi: 2, z_lo: 2; z = z_hi * 2 + z_lo), core: 2. Of those that a mesh axis runs over, the one named last changes fastest.
Arguments:
- vectors: bfloat16 [16384, 256], P(('row', 'col')), may hold values from -6 to 6
- blocks: bfloat16 [8, 16, 256, 128, 128], P('row', 'col'), may hold values from -0.03125 to 0.03125
- block_rows: int32 [8, 16, 256], P('row', 'col'), may hold values from 0 to 15
- block_cols: int32 [8, 16, 256], P('row', 'col'), may hold values from 0 to 7
- counts: int32 [8, 16], P('row', 'col'), may hold values from 1 to 256, as said below
Outputs:
- filtered: bfloat16 [16384, 256], P(('row', 'col'))
- gram: float32 [256, 256], P(('row', 'col'))
The draws below stay inside these ranges and needn't reach their ends.
Inputs may be any that keep to these rules, and one draw needn't show every extreme that they name: Entries of a tile at positions counts[r, c] and beyond are padding; some tile stores exactly 256 blocks.
All inputs are finite; a program needn't handle non-finite values.
Results may differ from the reference program's by a relative error of at most 0.017.
Values may be sent and summed in bfloat16 or wider, within the bound.
No kernel may reach another device: no remote copies, remote signals or barrier semaphores. Data moves between devices by JAX's collectives and lax.ppermute only.
A program may use at most 64 MiB of HBM per device.

```python
import jax
import jax.numpy as jnp
from jax import lax

BLOCK = 128
VECS = 256
BR = 16
MAXB = 256
DEG = 3
ORDER = 16384
COLBLK = 8
N_ROW = 8
N_COL = 16


def draw_counts(key, part):
    key = jax.random.fold_in(key, 11)
    key_level, key_jitter, key_pick, key_low = jax.random.split(key, 4)
    divisors = jnp.array([1, 2, 4, 8], jnp.int32)
    levels = jax.random.randint(key_level, (N_ROW, N_COL), 0, 4)
    ceiling = jnp.maximum(MAXB // divisors[levels], 1)
    jitter = jax.random.randint(key_jitter, (N_ROW, N_COL), 0, ceiling // 2 + 1)
    stored = jnp.maximum(ceiling - jitter, 1)
    tiles = N_ROW * N_COL
    chosen = jax.random.randint(key_pick, (), 0, tiles)
    lowest = (chosen + 1 + jax.random.randint(key_low, (), 0, tiles - 1)) % tiles
    positions = jnp.arange(tiles)
    flattened = stored.reshape(-1)
    flattened = jnp.where(positions == lowest, 1, flattened)
    flattened = jnp.where(positions == chosen, MAXB, flattened)
    return flattened.reshape(N_ROW, N_COL).astype(jnp.int32)


def place_ends(entries, stream_key, low, largest):
    place = [jax.random.randint(jax.random.fold_in(stream_key, axis), (), 0, length) for axis, length in enumerate(entries.shape)]
    longest = entries.shape.index(max(entries.shape))
    neighbour = place[:longest] + [(place[longest] + 1) % entries.shape[longest]] + place[longest + 1:]
    return entries.at[tuple(place)].set(low).at[tuple(neighbour)].set(largest)


def block_scale(stream_key, shape, cuts, least, largest):
    gain = 1.0
    for dim, shards_of in cuts:
        heights = jax.random.uniform(jax.random.fold_in(jax.random.fold_in(stream_key, 6), dim), (shards_of,), jnp.float32, least / len(cuts), largest / len(cuts))
        gain = gain * jnp.repeat(jnp.exp(heights), shape[dim] // shards_of).reshape((-1,) + (1,) * (len(shape) - 1 - dim))
    return gain


def bell_draw(rng, dims, deviation, limit, shards=(), held_as=jnp.bfloat16):
    entries = jax.random.normal(rng, dims, jnp.float32) * deviation
    if len(shards) > 0:
        entries = block_scale(rng, dims, shards, -0.22, 0.18) * entries
    return jnp.clip(entries, min=-limit, max=limit).astype(held_as)


def setup_inputs(seed: int = 0) -> dict:
    key_of = jax.random.split(jax.random.key(seed), 6)
    return {
        "vectors": bell_draw(key_of[0], (ORDER, VECS), 1.0, 6.0, ((0, 128),)),
        "blocks": bell_draw(key_of[1], (N_ROW, N_COL, MAXB, BLOCK, BLOCK), (BLOCK * N_COL * MAXB // BR) ** -0.5, 0.03125, ((0, 8), (1, 16))),
        "block_rows": place_ends(jax.random.randint(key_of[2], (N_ROW, N_COL, MAXB), 0, BR), jax.random.fold_in(key_of[2], 1), 0, BR - 1).astype(jnp.int32),
        "block_cols": place_ends(jax.random.randint(key_of[3], (N_ROW, N_COL, MAXB), 0, COLBLK), jax.random.fold_in(key_of[3], 1), 0, COLBLK - 1).astype(jnp.int32),
        "counts": draw_counts(jax.random.fold_in(key_of[5], 71), 0),
    }


def product(current, blocks, block_rows, block_cols, counts):
    column_sets = current.reshape(ORDER // (8 * N_COL), N_COL, 8, VECS).transpose(1, 0, 2, 3)
    column_sets = column_sets.reshape(N_COL, COLBLK, BLOCK, VECS)
    entry_index = jnp.arange(MAXB, dtype=jnp.int32)

    def grid_row(row_id):
        def grid_tile(col_id):
            pieces = jnp.take(column_sets[col_id], block_cols[row_id, col_id], axis=0)
            products = jnp.einsum("eab,ebk->eak", blocks[row_id, col_id].astype(jnp.float32), pieces.astype(jnp.float32))
            active_entries = entry_index < counts[row_id, col_id]
            products = jnp.where(active_entries[:, None, None], products, jnp.zeros_like(products))
            summed = jax.ops.segment_sum(products, block_rows[row_id, col_id], num_segments=BR)
            return summed.astype(jnp.bfloat16)

        tile_terms = lax.map(grid_tile, jnp.arange(N_COL, dtype=jnp.int32))
        return jnp.sum(tile_terms.astype(jnp.float32), axis=0)

    bands = lax.map(grid_row, jnp.arange(N_ROW, dtype=jnp.int32))
    return bands.reshape(ORDER, VECS)


def reference(vectors, blocks, block_rows, block_cols, counts):
    previous = vectors
    current = vectors
    for degree in range(DEG):
        summed = product(current, blocks, block_rows, block_cols, counts)
        if degree == 0:
            updated = summed.astype(jnp.bfloat16)
        else:
            updated = (2.0 * summed - previous.astype(jnp.float32)).astype(jnp.bfloat16)
        previous, current = current, updated
    gram = jnp.dot(current.T, current, preferred_element_type=jnp.float32) / (BR * BLOCK // N_COL)
    return current, gram
```

```python
import functools

import jax
import jax.numpy as jnp
from jax import lax
from jax.experimental import pallas as pl
from jax.experimental.pallas import tpu as pltpu
from jax.sharding import PartitionSpec as P

BLOCK = 128
BR = 16
COLBLK = 8
MAXB = 256
DEG = 3
RUN = 8
CHUNK = 16
UNROLL = 4
VMEM_LIMIT = 48 * 1024 * 1024


def merge_kernel(rows_ref, cols_ref, stored_ref, blocks_ref, out_ref, held, total, sems):
    stored = stored_ref[0]
    chunks = MAXB // CHUNK

    def copy(g):
        part = pl.ds(g * CHUNK, CHUNK)
        return pltpu.make_async_copy(blocks_ref.at[part], held.at[part], sems.at[g])

    for g in range(chunks):

        @pl.when(g * CHUNK < stored)
        def _():
            copy(g).start()

    @pl.loop(0, COLBLK)
    def _(j):
        total[j] = jnp.zeros(total.shape[1:], total.dtype)

    @pl.loop(0, (stored + CHUNK - 1) // CHUNK)
    def _(g):
        copy(g).wait()

        @pl.loop(0, CHUNK // UNROLL)
        def _(u):
            for k in range(UNROLL):
                e = g * CHUNK + u * UNROLL + k
                col = jnp.where(e < stored, cols_ref[e], COLBLK)
                part = pl.ds(pl.multiple_of(rows_ref[e] * RUN, RUN), RUN)
                block = held[e].astype(jnp.float32).reshape(BLOCK // RUN, RUN, BLOCK)
                total[col, :, part, :] = total[col, :, part, :] + block

    for j in range(COLBLK):
        out_ref[:, j * BLOCK : (j + 1) * BLOCK] = (
            total[j].reshape(BR * BLOCK, BLOCK).astype(out_ref.dtype)
        )


def merge(tile_rows, tile_cols, stored, tile_blocks):
    smem = pl.BlockSpec(memory_space=pltpu.SMEM)
    return pl.pallas_call(
        merge_kernel,
        out_shape=jax.ShapeDtypeStruct((BR * BLOCK, COLBLK * BLOCK), jnp.bfloat16),
        in_specs=[smem, smem, smem, pl.BlockSpec(memory_space=pl.ANY)],
        out_specs=pl.BlockSpec(memory_space=pltpu.VMEM),
        scratch_shapes=[
            pltpu.VMEM((MAXB, BLOCK, BLOCK), jnp.bfloat16),
            pltpu.VMEM((COLBLK + 1, BLOCK // RUN, BR * RUN, BLOCK), jnp.float32),
            pltpu.SemaphoreType.DMA((MAXB // CHUNK,)),
        ],
        compiler_params=pltpu.CompilerParams(vmem_limit_bytes=VMEM_LIMIT),
        cost_estimate=pl.CostEstimate(
            flops=MAXB * BLOCK * BLOCK,
            bytes_accessed=(MAXB + BR * COLBLK) * BLOCK * BLOCK * 2,
            transcendentals=0,
        ),
        name="merge_blocks",
    )(tile_rows, tile_cols, stored, tile_blocks)


def product_kernel(tile_ref, panel_ref, out_ref):
    step = 512

    @pl.loop(0, tile_ref.shape[0] // step)
    def _(m):
        part = pl.ds(pl.multiple_of(m * step, step), step)
        out_ref[part, :] = jnp.dot(
            tile_ref[part, :], panel_ref[...], preferred_element_type=jnp.float32
        ).astype(out_ref.dtype)


def last_product_kernel(col_ref, tile_ref, panel_ref, held_ref, out_ref, total):
    step = 512

    @pl.loop(0, tile_ref.shape[0] // step)
    def _(m):
        part = pl.ds(pl.multiple_of(m * step, step), step)
        total[part, :] = jnp.dot(
            tile_ref[part, :], panel_ref[...], preferred_element_type=jnp.float32
        )

    mine = pl.ds(pl.multiple_of(col_ref[0] * BLOCK, BLOCK), BLOCK)
    total[mine, :] = total[mine, :] - 0.5 * held_ref[...].astype(jnp.float32)

    @pl.loop(0, BR)
    def _(i):
        runs = [
            total[pl.ds(pl.multiple_of(j * BLOCK + i * RUN, RUN), RUN), :]
            for j in range(BLOCK // RUN)
        ]
        out_ref[pl.ds(pl.multiple_of(i * BLOCK, BLOCK), BLOCK), :] = jnp.concatenate(
            runs, axis=0
        ).astype(out_ref.dtype)


def product(tile, panel, col=None, held=None):
    vmem = pl.BlockSpec(memory_space=pltpu.VMEM)
    width = panel.shape[1]
    last = held is not None
    out_shape = (tile.shape[0], width)
    return pl.pallas_call(
        last_product_kernel if last else product_kernel,
        out_shape=jax.ShapeDtypeStruct(out_shape, jnp.bfloat16),
        in_specs=[pl.BlockSpec(memory_space=pltpu.SMEM), vmem, vmem, vmem] if last else [vmem, vmem],
        out_specs=vmem,
        scratch_shapes=[pltpu.VMEM(out_shape, jnp.float32)] if last else [],
        compiler_params=pltpu.CompilerParams(vmem_limit_bytes=VMEM_LIMIT),
        cost_estimate=pl.CostEstimate(
            flops=2 * tile.shape[0] * tile.shape[1] * width,
            bytes_accessed=2 * (tile.size + panel.size + tile.shape[0] * width),
            transcendentals=0,
        ),
        name="last_product" if last else "tile_product",
    )(*((col, tile, panel, held) if last else (tile, panel)))


def per_device(vectors, blocks, block_rows, block_cols, counts):
    col_count = lax.axis_size("col")
    row_count = lax.axis_size("row")
    shard_rows, width = vectors.shape
    col = lax.axis_index("col").astype(jnp.int32).reshape(1)

    def exchange(parts, axes):
        return lax.all_to_all(parts, axes, split_axis=0, concat_axis=0, tiled=True)

    def gather(own):
        copies = jnp.broadcast_to(own[None], (row_count,) + own.shape)
        return exchange(copies, "row").reshape(row_count * shard_rows, width)

    def reduce(terms):
        arrived = exchange(terms.reshape(col_count, shard_rows, width), "col")
        return jnp.sum(arrived.astype(jnp.float32), axis=0)

    with jax.named_scope("merge"):
        tile = merge(block_rows[0, 0], block_cols[0, 0], counts[0], blocks[0, 0])
    with jax.named_scope("deal"):
        runs = vectors.reshape(col_count, RUN, width)
        dealt = exchange(runs, "col").reshape(shard_rows, width)
    with jax.named_scope("gather0"):
        panel = gather(dealt)
    with jax.named_scope("step1"):
        first = reduce(product(tile, panel)).astype(jnp.bfloat16)
        panel = gather(first)
    with jax.named_scope("step2"):
        summed = reduce(product(tile, panel))
        second = (2.0 * summed - dealt.astype(jnp.float32)).astype(jnp.bfloat16)
        panel = gather(second)
    with jax.named_scope("step3"):
        filtered = (2.0 * reduce(product(tile, panel, col, first))).astype(jnp.bfloat16)
    with jax.named_scope("gram"):
        local = jnp.dot(filtered.T, filtered, preferred_element_type=jnp.float32)
        devices = row_count * col_count
        arrived = exchange(local.reshape(devices, width // devices, width), ("row", "col"))
        gram = jnp.sum(arrived, axis=0) / (BR * BLOCK // col_count)
    return filtered, gram


def solution(mesh):
    in_specs = (
        P(("row", "col"), None),
        P("row", "col", None, None, None),
        P("row", "col", None),
        P("row", "col", None),
        P("row", "col"),
    )
    out_specs = (P(("row", "col"), None), P(("row", "col"), None))
    return jax.shard_map(
        per_device, mesh=mesh, in_specs=in_specs, out_specs=out_specs, check_vma=False
    )
```

```python
import functools

import jax
import jax.numpy as jnp
from jax import lax
from jax.experimental import pallas as pl
from jax.experimental.pallas import tpu as pltpu
from jax.sharding import PartitionSpec as P

BLOCK = 128
BR = 16
COLBLK = 8
MAXB = 256
RUN = 8
HALF = 8
QUARTER = HALF * HALF * RUN
PAIR = 2 * BLOCK
CHUNK = 16
UNROLL = 4
MERGE_VMEM = 64 * 1024 * 1024 - 4096
SMALL_VMEM = 8 * 1024 * 1024
VMEM = pl.BlockSpec(memory_space=pltpu.VMEM)
HBM = pl.BlockSpec(memory_space=pltpu.HBM)
F32 = jnp.float32
BF16 = jnp.bfloat16


def small_call(kernel, name, out_shapes, operands, scratch=(), flops=0):
    outs = [jax.ShapeDtypeStruct(shape, BF16) for shape in out_shapes]
    sizes = sum(x.size for x in operands) + sum(x.size for x in outs)
    return pl.pallas_call(
        kernel,
        out_shape=outs,
        in_specs=[VMEM] * len(operands),
        out_specs=[VMEM] * len(outs),
        scratch_shapes=list(scratch),
        compiler_params=pltpu.CompilerParams(vmem_limit_bytes=SMALL_VMEM),
        cost_estimate=pl.CostEstimate(
            flops=flops, bytes_accessed=2 * sizes, transcendentals=0
        ),
        name=name,
    )(*operands)


def merge_kernel(rows_ref, cols_ref, stored_ref, blocks_ref, *refs):
    tiles, (rows, cols, stored, held, total, done, index_sems, sems, tile_sems) = (
        refs[:4],
        refs[4:],
    )
    row_id, core = lax.axis_index("row"), lax.axis_index("col") & 1
    chunks = MAXB // CHUNK
    indices = [
        pltpu.make_async_copy(source, target, index_sems.at[k])
        for k, (source, target) in enumerate(
            ((stored_ref, stored), (rows_ref, rows), (cols_ref, cols))
        )
    ]

    def copy(g):
        part = pl.ds(g * CHUNK, CHUNK)
        return pltpu.make_async_copy(blocks_ref.at[part], held.at[part], sems.at[g])

    for index in indices:
        index.start()
    for g in range(chunks):
        copy(g).start()

    @pl.loop(0, COLBLK)
    def _(j):
        total[j] = jnp.zeros(total.shape[1:], total.dtype)

    for index in indices:
        index.wait()
    count = stored[0]

    @pl.loop(0, chunks)
    def _(g):
        copy(g).wait()

        @pl.when(g * CHUNK < count)
        def _():
            @pl.loop(0, CHUNK // UNROLL)
            def _(u):
                for k in range(UNROLL):
                    e = g * CHUNK + u * UNROLL + k
                    col = cols[e]
                    col = ((col // 2 - row_id // 2) & 3) * 2 + ((col ^ row_id) & 1)
                    col = jnp.where(e < count, col, COLBLK)
                    row = rows[e]
                    part = pl.ds(pl.multiple_of(row // 2 * RUN, RUN), RUN)
                    block = held[e].astype(F32).reshape(HALF, 2, RUN, BLOCK)
                    place = (col, row & 1, slice(None), slice(None), part, slice(None))
                    total[place] = total[place] + block

    out = []
    for p in range(2):
        for i in range(2):
            target, source = abs(1 - p - core), abs(1 - i - core)
            tile = done.at[i] if p else tiles[i]
            for j in range(COLBLK):
                terms = total[j, source, :, target]
                tile[:, j * BLOCK : (j + 1) * BLOCK] = (
                    terms.reshape(QUARTER, BLOCK).astype(done.dtype)
                )
            if p:
                out.append(pltpu.make_async_copy(tile, tiles[2 + i], tile_sems.at[i]))
                out[-1].start()
    for copied in out:
        copied.wait()


def merge(tile_rows, tile_cols, stored, tile_blocks):
    quarter = jax.ShapeDtypeStruct((QUARTER, COLBLK * BLOCK), BF16)
    return pl.pallas_call(
        merge_kernel,
        out_shape=[quarter] * 4,
        in_specs=[HBM] * 4,
        out_specs=[VMEM, VMEM, HBM, HBM],
        scratch_shapes=[
            pltpu.SMEM((MAXB,), jnp.int32),
            pltpu.SMEM((MAXB,), jnp.int32),
            pltpu.SMEM((1,), jnp.int32),
            pltpu.VMEM((MAXB, BLOCK, BLOCK), BF16),
            pltpu.VMEM((COLBLK + 1, 2, HALF, 2, HALF * RUN, BLOCK), F32),
            pltpu.VMEM((2,) + quarter.shape, BF16),
            pltpu.SemaphoreType.DMA((3,)),
            pltpu.SemaphoreType.DMA((MAXB // CHUNK,)),
            pltpu.SemaphoreType.DMA((2,)),
        ],
        compiler_params=pltpu.CompilerParams(vmem_limit_bytes=60 * 1024 * 1024),
        cost_estimate=pl.CostEstimate(
            flops=MAXB * BLOCK * BLOCK,
            bytes_accessed=(MAXB + BR * COLBLK) * BLOCK * BLOCK * 2,
            transcendentals=0,
        ),
        name="merge_blocks",
    )(tile_rows, tile_cols, stored, tile_blocks)


def copies_kernel(own_ref, out_ref, held, own_sem, sems):
    load = pltpu.make_async_copy(own_ref, held, own_sem)
    load.start()
    load.wait()
    stores = [
        pltpu.make_async_copy(held, out_ref.at[k], sems.at[k]) for k in range(out_ref.shape[0])
    ]
    for store in stores:
        store.start()
    for store in stores:
        store.wait()


def copies(own, count):
    return pl.pallas_call(
        copies_kernel,
        out_shape=jax.ShapeDtypeStruct((count,) + own.shape, own.dtype),
        in_specs=[HBM],
        out_specs=HBM,
        scratch_shapes=[
            pltpu.VMEM(own.shape, own.dtype),
            pltpu.SemaphoreType.DMA,
            pltpu.SemaphoreType.DMA((count,)),
        ],
        compiler_params=pltpu.CompilerParams(vmem_limit_bytes=MERGE_VMEM),
        name="copies",
    )(own)


def dot(a, b):
    return jnp.dot(a, b, preferred_element_type=F32)


def put_together(part_refs, panel):
    rows = panel.shape[0] // len(part_refs)
    for k, part_ref in enumerate(part_refs):
        panel[k * rows : (k + 1) * rows, :] = part_ref[...]


def step_kernel(keep, first, *refs):
    tiles, refs = refs[:2], refs[2:]
    row_id, col_id = lax.axis_index("row"), lax.axis_index("col")
    core = col_id & 1
    if first:
        dealt_ref, out_ref, panel, total = refs[0], refs[1], refs[-2], refs[-1]
        for k in range(COLBLK):
            part = ((row_id // 2 + k // 2) & 3) * 2 + ((row_id ^ k) & 1)
            part = pl.ds(pl.multiple_of(part * BLOCK, BLOCK), BLOCK)
            panel[k * BLOCK : (k + 1) * BLOCK, :] = dealt_ref[part, :]
        if not keep:
            refs[2][...] = panel[:PAIR, :]
    else:
        out_ref, panel, total = refs[4:]
        put_together(refs[:4], panel)
    for i in range(2):
        terms = dot(tiles[i][...], panel[...])
        terms = terms.reshape(HALF, HALF, RUN, terms.shape[1])
        for t in range(HALF):
            away = ((t // 2 - col_id // 4) & 3) * 2 + ((t ^ (col_id // 2)) & 1)
            total[away, :, core if i else 1 - core] = terms[t]
    out_ref[...] = total[...].reshape(out_ref.shape).astype(out_ref.dtype)


def last_kernel(keep, *refs):
    tiles, parts, (first_ref, out_ref, panel, total) = refs[:2], refs[2:6], refs[6:]
    put_together(parts, panel)
    col_id = lax.axis_index("col")
    core = col_id & 1
    for j in range(2):
        terms = dot(tiles[j][...], panel[...])
        terms = terms.reshape(HALF, HALF, RUN, terms.shape[1])
        for t in range(HALF):
            total[:, t, core if j else 1 - core] = terms[t]
    first = first_ref[:BLOCK, :].astype(F32).reshape(HALF, 2, RUN, first_ref.shape[1])
    target = core if keep else 1 - core
    first = jnp.where(target == 0, first[:, 0], first[:, 1])
    mine = col_id // 2
    total[:, mine, core] = total[:, mine, core] - 0.5 * first
    out_ref[...] = total[...].reshape(out_ref.shape).astype(out_ref.dtype)


def add_kernel(a_ref, b_ref, *out_refs):
    rows = out_refs[0].shape[0]
    for k, out_ref in enumerate(out_refs):
        part = slice(k * rows, (k + 1) * rows)
        out_ref[...] = (a_ref[part, :].astype(F32) + b_ref[part, :].astype(F32)).astype(BF16)


def sum_kernel(a_ref, b_ref, c_ref, d_ref, *out_refs):
    rows = out_refs[0].shape[0]
    for k, out_ref in enumerate(out_refs):
        part = slice(k * rows, (k + 1) * rows)
        terms = [ref[part, :].astype(F32) for ref in (a_ref, b_ref, c_ref, d_ref)]
        out_ref[...] = ((terms[0] + terms[1]) + (terms[2] + terms[3])).astype(BF16)


def next_kernel(scale, own_ref, arrived_ref, near_ref, far_ref, *refs):
    out_ref = refs[-1]
    pairs = ((own_ref, arrived_ref), (near_ref, far_ref))
    for k, (a_ref, b_ref) in enumerate(pairs):
        part = slice(k * BLOCK, (k + 1) * BLOCK)
        summed = a_ref[...].astype(F32) + b_ref[...].astype(F32)
        if len(refs) > 1:
            summed = scale * summed - refs[0][part, :].astype(F32)
        out_ref[part, :] = summed.astype(BF16)


def per_device(vectors, blocks, block_rows, block_cols, counts):
    col_count = lax.axis_size("col")
    row_count = lax.axis_size("row")
    devices = row_count * col_count
    shard_rows, width = vectors.shape
    half_rows = 2 * QUARTER
    flops = 2 * half_rows * COLBLK * BLOCK * width

    def exchange(parts, axes, groups=None):
        return lax.all_to_all(
            parts, axes, split_axis=0, concat_axis=0, tiled=True, axis_index_groups=groups
        )

    def other_core(x):
        return lax.ppermute(x, "col", [(i, i ^ 1) for i in range(col_count)])

    def along_x(x, k):
        return lax.ppermute(x, "col", [(i, (i + 4 * k) % col_count) for i in range(col_count)])

    def along_y(x, k):
        return lax.ppermute(x, "row", [(i, (i + 2 * k) % row_count) for i in range(row_count)])

    def near_z(x):
        return lax.ppermute(x, "row", [(i, i ^ 1) for i in range(row_count)])

    def far_z(x):
        return lax.ppermute(x, "col", [(i, i ^ 2) for i in range(col_count)])

    def both_z(x):
        pairs = [
            (r * col_count + c, (r ^ 1) * col_count + (c ^ 2))
            for r in range(row_count)
            for c in range(col_count)
        ]
        return lax.ppermute(x, ("row", "col"), pairs)

    scratch = [
        pltpu.VMEM((COLBLK * BLOCK, width), BF16),
        pltpu.VMEM((HALF, HALF, 2, RUN, width), F32),
    ]

    def step(tiles, parts, first, previous):
        wide = (half_rows, width)
        sent, *pair = small_call(
            functools.partial(step_kernel, False, first),
            "send",
            [wide] + ([(PAIR, width)] if first else []),
            (tiles[0], tiles[1]) + parts,
            scratch,
            flops,
        )
        previous = pair[0] if first else previous
        arrived = other_core(sent)
        (kept,) = small_call(
            functools.partial(step_kernel, True, first),
            "keep",
            [wide],
            (tiles[2], tiles[3]) + parts,
            scratch,
            flops,
        )
        terms = small_call(add_kernel, "add", [(PAIR, width)] * 4, (kept, arrived))
        arrived = [along_x(terms[k], k) for k in (2, 1, 3)]
        own, other = small_call(
            sum_kernel, "sum_x", [(BLOCK, width)] * 2, (terms[0], *arrived)
        )
        arrived, far, near = far_z(other), both_z(other), near_z(own)
        operands = (own, arrived, near, far) + (() if first else (previous,))
        (pair,) = small_call(
            functools.partial(next_kernel, 2.0), "next", [(PAIR, width)], operands
        )
        sides = {k: along_y(pair, k) for k in (2, 1, 3)}
        return (pair, sides[3], sides[2], sides[1]), previous

    with jax.named_scope("merge"):
        tiles = merge(block_rows[0, 0], block_cols[0, 0], counts[0], blocks[0, 0])
    with jax.named_scope("deal"):
        panel = exchange(copies(vectors, row_count).reshape(devices, RUN, width), ("row", "col"))
        panel = panel.reshape(row_count * shard_rows, width)
    with jax.named_scope("step1"):
        parts, previous = step(tiles, (panel,), True, None)
        first = parts[0]
    with jax.named_scope("step2"):
        parts, _ = step(tiles, parts, False, previous)
    with jax.named_scope("step3"):
        halves = []
        for keep in (False, True):
            (half,) = small_call(
                functools.partial(last_kernel, keep),
                "last_keep" if keep else "last_send",
                [(half_rows, width)],
                (tiles[int(keep)], tiles[2 + int(keep)]) + parts + (first,),
                scratch,
                flops,
            )
            halves.append(half if keep else other_core(half))
        (terms,) = small_call(add_kernel, "add", [(half_rows, width)], tuple(halves))
        same_core = [list(range(c, col_count, 2)) for c in range(2)]
        arrived = exchange(terms.reshape(HALF, shard_rows, width), "col", same_core)
        summed = jnp.sum(arrived.astype(F32), axis=0)
        filtered = (2.0 * summed).astype(BF16)
    with jax.named_scope("gram"):
        local = dot(filtered.T, filtered).astype(BF16)
        arrived = exchange(local.reshape(devices, width // devices, width), ("row", "col"))
        gram = jnp.sum(arrived.astype(F32), axis=0) / (BR * BLOCK // col_count)
    return filtered, gram


def solution(mesh):
    in_specs = (
        P(("row", "col"), None),
        P("row", "col", None, None, None),
        P("row", "col", None),
        P("row", "col", None),
        P("row", "col"),
    )
    out_specs = (P(("row", "col"), None), P(("row", "col"), None))
    return jax.shard_map(
        per_device, mesh=mesh, in_specs=in_specs, out_specs=out_specs, check_vma=False
    )
```

```python
import functools

import jax
import jax.numpy as jnp
from jax import lax
from jax.experimental import pallas as pl
from jax.experimental.pallas import tpu as pltpu
from jax.sharding import PartitionSpec as P

BLOCK = 128
BR = 16
COLBLK = 8
MAXB = 256
RUN = 8
HALF = 8
QUARTER = HALF * HALF * RUN
PAIR = 2 * BLOCK
CHUNK = 16
UNROLL = 16
PIECES = 4
MERGE_VMEM = 60 * 1024 * 1024
SMALL_VMEM = 8 * 1024 * 1024
PRODUCT_VMEM = 50 * 1024 * 1024
ROOM = 16
VMEM = pl.BlockSpec(memory_space=pltpu.VMEM)
HBM = pl.BlockSpec(memory_space=pltpu.HBM)
F32 = jnp.float32
BF16 = jnp.bfloat16


def small_call(kernel, name, out_shapes, operands, scratch=(), flops=0, tile=None):
    tiles = [] if tile is None else [tile]
    outs = [jax.ShapeDtypeStruct(shape, BF16) for shape in out_shapes]
    sizes = sum(x.size for x in operands) + sum(x.size for x in outs)
    return pl.pallas_call(
        kernel,
        out_shape=outs,
        in_specs=[HBM] * len(tiles) + [VMEM] * len(operands),
        out_specs=[VMEM] * len(outs),
        scratch_shapes=list(scratch),
        compiler_params=pltpu.CompilerParams(vmem_limit_bytes=PRODUCT_VMEM if tiles else SMALL_VMEM),
        cost_estimate=pl.CostEstimate(
            flops=flops, bytes_accessed=2 * sizes, transcendentals=0
        ),
        name=name,
    )(*tiles, *operands)


def merge_kernel(
    rows_ref, cols_ref, stored_ref, blocks_ref, tile_ref,
    rows, cols, stored, held, total, done, index_sems, sems, tile_sems,
):
    row_id, core = lax.axis_index("row"), lax.axis_index("col") & 1
    chunks = MAXB // CHUNK
    indices = [
        pltpu.make_async_copy(source, target, index_sems.at[k])
        for k, (source, target) in enumerate(
            ((stored_ref, stored), (rows_ref, rows), (cols_ref, cols))
        )
    ]

    def copy(g):
        part = pl.ds(g * CHUNK, CHUNK)
        return pltpu.make_async_copy(blocks_ref.at[part], held.at[part], sems.at[g])

    for index in indices:
        index.start()
    for g in range(chunks):
        copy(g).start()

    @pl.loop(0, COLBLK)
    def _(j):
        total[j] = jnp.zeros(total.shape[1:], total.dtype)

    for index in indices:
        index.wait()
    count = stored[0]

    @pl.loop(0, chunks)
    def _(g):
        copy(g).wait()

        @pl.when(g * CHUNK < count)
        def _():
            @pl.loop(0, CHUNK // UNROLL)
            def _(u):
                for k in range(UNROLL):
                    e = g * CHUNK + u * UNROLL + k
                    col = cols[e]
                    col = ((col // 2 - row_id // 2) & 3) * 2 + ((col ^ row_id) & 1)
                    col = jnp.where(e < count, col, COLBLK)
                    row = rows[e]
                    part = pl.ds(pl.multiple_of(row // 2 * RUN, RUN), RUN)
                    block = held[e].astype(F32).reshape(HALF, 2, RUN, BLOCK)
                    place = (col, row & 1, slice(None), slice(None), part, slice(None))
                    total[place] = total[place] + block

    out = []
    for p in range(2):
        for i in range(2):
            target, source = abs(1 - p - core), abs(1 - i - core)
            k = 2 * p + i
            for j in range(COLBLK):
                terms = total[j, source, :, target]
                done[k, :, j * BLOCK : (j + 1) * BLOCK] = (
                    terms.reshape(QUARTER, BLOCK).astype(done.dtype)
                )
            out.append(pltpu.make_async_copy(done.at[k], tile_ref.at[k], tile_sems.at[k]))
            out[-1].start()
    for copied in out:
        copied.wait()


def merge(tile_rows, tile_cols, stored, tile_blocks):
    quarter = (QUARTER, COLBLK * BLOCK)
    return pl.pallas_call(
        merge_kernel,
        out_shape=jax.ShapeDtypeStruct((ROOM,) + quarter, BF16),
        in_specs=[HBM] * 4,
        out_specs=HBM,
        scratch_shapes=[
            pltpu.SMEM((MAXB,), jnp.int32),
            pltpu.SMEM((MAXB,), jnp.int32),
            pltpu.SMEM((1,), jnp.int32),
            pltpu.VMEM((MAXB, BLOCK, BLOCK), BF16),
            pltpu.VMEM((COLBLK + 1, 2, HALF, 2, HALF * RUN, BLOCK), F32),
            pltpu.VMEM((4,) + quarter, BF16),
            pltpu.SemaphoreType.DMA((3,)),
            pltpu.SemaphoreType.DMA((MAXB // CHUNK,)),
            pltpu.SemaphoreType.DMA((4,)),
        ],
        compiler_params=pltpu.CompilerParams(vmem_limit_bytes=MERGE_VMEM),
        cost_estimate=pl.CostEstimate(
            flops=MAXB * BLOCK * BLOCK,
            bytes_accessed=(MAXB + BR * COLBLK) * BLOCK * BLOCK * 2,
            transcendentals=0,
        ),
        name="merge_blocks",
    )(tile_rows, tile_cols, stored, tile_blocks)


def copies_kernel(own_ref, out_ref, held, own_sem, sems):
    load = pltpu.make_async_copy(own_ref, held, own_sem)
    load.start()
    load.wait()
    stores = [
        pltpu.make_async_copy(held, out_ref.at[k], sems.at[k]) for k in range(out_ref.shape[0])
    ]
    for store in stores:
        store.start()
    for store in stores:
        store.wait()


def copies(own, count):
    return pl.pallas_call(
        copies_kernel,
        out_shape=jax.ShapeDtypeStruct((count,) + own.shape, own.dtype),
        in_specs=[HBM],
        out_specs=HBM,
        scratch_shapes=[
            pltpu.VMEM(own.shape, own.dtype),
            pltpu.SemaphoreType.DMA,
            pltpu.SemaphoreType.DMA((count,)),
        ],
        compiler_params=pltpu.CompilerParams(vmem_limit_bytes=MERGE_VMEM),
        name="copies",
    )(own)


def dot(a, b):
    return jnp.dot(a, b, preferred_element_type=F32)


def put_together(part_refs, panel):
    rows = panel.shape[0] // len(part_refs)
    for k, part_ref in enumerate(part_refs):
        panel[k * rows : (k + 1) * rows, :] = part_ref[...]


def fetch_kernel(halves, tile_ref, *refs):
    *out_refs, sems = refs[-1 - len(halves) :]
    rows = QUARTER // PIECES
    copies = []
    for h, (out_ref, half) in enumerate(zip(out_refs, halves)):
        for q, quarter in enumerate(half):
            for k in range(PIECES):
                part = pl.ds(k * rows, rows)
                copies.append(
                    pltpu.make_async_copy(
                        tile_ref.at[quarter, part], out_ref.at[q, part], sems.at[h, q, k]
                    )
                )
                copies[-1].start()
    for copy in copies:
        copy.wait()


def step_kernel(first, keep, *refs):
    tile_ref, refs = refs[0], refs[1:]
    refs, (panel, total) = refs[:-2], refs[-2:]
    row_id, col_id = lax.axis_index("row"), lax.axis_index("col")
    core = col_id & 1
    if first:
        dealt_ref, out_ref = refs[:2]
        for k in range(COLBLK):
            part = ((row_id // 2 + k // 2) & 3) * 2 + ((row_id ^ k) & 1)
            part = pl.ds(pl.multiple_of(part * BLOCK, BLOCK), BLOCK)
            panel[k * BLOCK : (k + 1) * BLOCK, :] = dealt_ref[part, :]
        if not keep:
            refs[2][...] = panel[:PAIR, :]
    else:
        out_ref = refs[4]
        put_together(refs[:4], panel)
    for i in range(2):
        terms = dot(tile_ref[i], panel[...])
        terms = terms.reshape(HALF, HALF, RUN, terms.shape[1])
        for t in range(HALF):
            away = ((t // 2 - col_id // 4) & 3) * 2 + ((t ^ (col_id // 2)) & 1)
            total[away, :, core if i else 1 - core] = terms[t]
    out_ref[...] = total[...].reshape(out_ref.shape).astype(out_ref.dtype)


def last_kernel(keep, tile_ref, *refs):
    parts, (first_ref, out_ref, panel, total) = refs[:4], refs[4:]
    put_together(parts, panel)
    col_id = lax.axis_index("col")
    core = col_id & 1
    for j in range(2):
        terms = dot(tile_ref[j], panel[...])
        terms = terms.reshape(HALF, HALF, RUN, terms.shape[1])
        for t in range(HALF):
            total[:, t, core if j else 1 - core] = terms[t]
    first = first_ref[:BLOCK, :].astype(F32).reshape(HALF, 2, RUN, first_ref.shape[1])
    target = core if keep else 1 - core
    first = jnp.where(target == 0, first[:, 0], first[:, 1])
    mine = col_id // 2
    total[:, mine, core] = total[:, mine, core] - 0.5 * first
    out_ref[...] = total[...].reshape(out_ref.shape).astype(out_ref.dtype)


def add_kernel(a_ref, b_ref, *out_refs):
    rows = out_refs[0].shape[0]
    for k, out_ref in enumerate(out_refs):
        part = slice(k * rows, (k + 1) * rows)
        out_ref[...] = (a_ref[part, :].astype(F32) + b_ref[part, :].astype(F32)).astype(BF16)


def sum_kernel(a_ref, b_ref, c_ref, d_ref, *out_refs):
    rows = out_refs[0].shape[0]
    for k, out_ref in enumerate(out_refs):
        part = slice(k * rows, (k + 1) * rows)
        terms = [ref[part, :].astype(F32) for ref in (a_ref, b_ref, c_ref, d_ref)]
        out_ref[...] = ((terms[0] + terms[1]) + (terms[2] + terms[3])).astype(BF16)


def next_kernel(scale, own_ref, arrived_ref, near_ref, far_ref, *refs):
    out_ref = refs[-1]
    pairs = ((own_ref, arrived_ref), (near_ref, far_ref))
    for k, (a_ref, b_ref) in enumerate(pairs):
        part = slice(k * BLOCK, (k + 1) * BLOCK)
        summed = a_ref[...].astype(F32) + b_ref[...].astype(F32)
        if len(refs) > 1:
            summed = scale * summed - refs[0][part, :].astype(F32)
        out_ref[part, :] = summed.astype(BF16)


def per_device(vectors, blocks, block_rows, block_cols, counts):
    col_count = lax.axis_size("col")
    row_count = lax.axis_size("row")
    devices = row_count * col_count
    shard_rows, width = vectors.shape
    half_rows = 2 * QUARTER
    flops = 2 * half_rows * COLBLK * BLOCK * width

    def exchange(parts, axes, groups=None):
        return lax.all_to_all(
            parts, axes, split_axis=0, concat_axis=0, tiled=True, axis_index_groups=groups
        )

    def other_core(x):
        return lax.ppermute(x, "col", [(i, i ^ 1) for i in range(col_count)])

    def along_x(x, k):
        return lax.ppermute(x, "col", [(i, (i + 4 * k) % col_count) for i in range(col_count)])

    def along_y(x, k):
        return lax.ppermute(x, "row", [(i, (i + 2 * k) % row_count) for i in range(row_count)])

    def near_z(x):
        return lax.ppermute(x, "row", [(i, i ^ 1) for i in range(row_count)])

    def far_z(x):
        return lax.ppermute(x, "col", [(i, i ^ 2) for i in range(col_count)])

    def both_z(x):
        pairs = [
            (r * col_count + c, (r ^ 1) * col_count + (c ^ 2))
            for r in range(row_count)
            for c in range(col_count)
        ]
        return lax.ppermute(x, ("row", "col"), pairs)

    scratch = [
        pltpu.VMEM((COLBLK * BLOCK, width), BF16),
        pltpu.VMEM((HALF, HALF, 2, RUN, width), F32),
    ]
    sems = pltpu.SemaphoreType.DMA((2, 2, PIECES))
    quarters = (2, QUARTER, COLBLK * BLOCK)

    def fetch(tile, *halves, after=()):
        kernel = functools.partial(fetch_kernel, halves)
        return small_call(kernel, "fetch", [quarters] * len(halves), after, [sems], 0, tile)

    def product(kernel, name, fetched, operands, more=()):
        wide = (half_rows, width)
        sent, *rest = small_call(
            functools.partial(kernel, False),
            name + "_send",
            [wide, *more],
            (fetched[0], *operands),
            scratch,
            flops,
        )
        arrived = other_core(sent)
        (kept,) = small_call(
            functools.partial(kernel, True),
            name + "_keep",
            [wide],
            (fetched[1], *operands),
            scratch,
            flops,
        )
        return (kept, arrived), rest

    def step(tile, fetched, parts, first, previous, which):
        kernel = functools.partial(step_kernel, first)
        more = [(PAIR, width)] if first else []
        terms, rest = product(kernel, "first" if first else "step", fetched, parts, more)
        terms = small_call(add_kernel, "add", [(PAIR, width)] * 4, terms)
        arrived = [along_x(terms[k], k) for k in (2, 1, 3)]
        fetched = fetch(tile, *which, after=(terms[0],))
        own, other = small_call(
            sum_kernel, "sum_x", [(BLOCK, width)] * 2, (terms[0], *arrived)
        )
        near, far, arrived = near_z(own), both_z(other), far_z(other)
        operands = (own, arrived, near, far) + (() if first else (previous,))
        (pair,) = small_call(
            functools.partial(next_kernel, 2.0), "next", [(PAIR, width)], operands
        )
        sides = {k: along_y(pair, k) for k in (1, 3, 2)}
        return (pair, sides[3], sides[2], sides[1]), fetched, (rest[0] if first else None)

    with jax.named_scope("merge"):
        tile = merge(block_rows[0, 0], block_cols[0, 0], counts[0], blocks[0, 0])
    with jax.named_scope("deal"):
        panel = exchange(copies(vectors, row_count).reshape(devices, RUN, width), ("row", "col"))
        panel = panel.reshape(row_count * shard_rows, width)
    with jax.named_scope("step1"):
        fetched = [*fetch(tile, (0, 1)), *fetch(tile, (2, 3))]
        parts, fetched, previous = step(tile, fetched, (panel,), True, None, ((0, 1), (2, 3)))
        first = parts[0]
    with jax.named_scope("step2"):
        parts, fetched, _ = step(tile, fetched, parts, False, previous, ((0, 2), (1, 3)))
    with jax.named_scope("step3"):
        terms, _ = product(last_kernel, "last", fetched, parts + (first,))
        (terms,) = small_call(add_kernel, "add", [(half_rows, width)], terms)
        same_core = [list(range(c, col_count, 2)) for c in range(2)]
        arrived = exchange(terms.reshape(HALF, shard_rows, width), "col", same_core)
        summed = jnp.sum(arrived.astype(F32), axis=0)
        filtered = (2.0 * summed).astype(BF16)
    with jax.named_scope("gram"):
        local = dot(filtered.T, filtered).astype(BF16)
        arrived = exchange(local.reshape(devices, width // devices, width), ("row", "col"))
        gram = jnp.sum(arrived.astype(F32), axis=0) / (BR * BLOCK // col_count)
    return filtered, gram


def solution(mesh):
    in_specs = (
        P(("row", "col"), None),
        P("row", "col", None, None, None),
        P("row", "col", None),
        P("row", "col", None),
        P("row", "col"),
    )
    out_specs = (P(("row", "col"), None), P(("row", "col"), None))
    return jax.shard_map(
        per_device, mesh=mesh, in_specs=in_specs, out_specs=out_specs, check_vma=False
    )
```

```python
import functools

import jax
import jax.numpy as jnp
from jax import lax
from jax.experimental import pallas as pl
from jax.experimental.pallas import tpu as pltpu
from jax.sharding import PartitionSpec as P

BLOCK = 128
BR = 16
COLBLK = 8
MAXB = 256
RUN = 8
HALF = 8
QUARTER = HALF * HALF * RUN
PAIR = 2 * BLOCK
CHUNK = 16
UNROLL = 16
PANEL_ORDER = (0, 2, 3, 1)
PIECES = 4
MERGE_VMEM = 60 * 1024 * 1024
SMALL_VMEM = 8 * 1024 * 1024
PRODUCT_VMEM = 50 * 1024 * 1024
ROOM = 16
VMEM = pl.BlockSpec(memory_space=pltpu.VMEM)
HBM = pl.BlockSpec(memory_space=pltpu.HBM)
F32 = jnp.float32
BF16 = jnp.bfloat16


def small_call(kernel, name, out_shapes, operands, scratch=(), flops=0, tile=None):
    tiles = [] if tile is None else [tile]
    outs = [jax.ShapeDtypeStruct(shape, BF16) for shape in out_shapes]
    sizes = sum(x.size for x in operands) + sum(x.size for x in outs)
    return pl.pallas_call(
        kernel,
        out_shape=outs,
        in_specs=[HBM] * len(tiles) + [VMEM] * len(operands),
        out_specs=[VMEM] * len(outs),
        scratch_shapes=list(scratch),
        compiler_params=pltpu.CompilerParams(vmem_limit_bytes=PRODUCT_VMEM if tiles else SMALL_VMEM),
        cost_estimate=pl.CostEstimate(
            flops=flops, bytes_accessed=2 * sizes, transcendentals=0
        ),
        name=name,
    )(*tiles, *operands)


def merge_kernel(
    rows_ref, cols_ref, stored_ref, blocks_ref, tile_ref,
    rows, cols, stored, held, total, done, index_sems, sems, tile_sems,
):
    row_id, core = lax.axis_index("row"), lax.axis_index("col") & 1
    chunks = MAXB // CHUNK
    indices = [
        pltpu.make_async_copy(source, target, index_sems.at[k])
        for k, (source, target) in enumerate(
            ((stored_ref, stored), (rows_ref, rows), (cols_ref, cols))
        )
    ]

    def copy(g):
        part = pl.ds(g * CHUNK, CHUNK)
        return pltpu.make_async_copy(blocks_ref.at[part], held.at[part], sems.at[g])

    for index in indices:
        index.start()
    for g in range(chunks):
        copy(g).start()

    @pl.loop(0, COLBLK)
    def _(j):
        total[j] = jnp.zeros(total.shape[1:], total.dtype)

    for index in indices:
        index.wait()
    count = stored[0]

    @pl.loop(0, chunks)
    def _(g):
        copy(g).wait()

        @pl.when(g * CHUNK < count)
        def _():
            @pl.loop(0, CHUNK // UNROLL)
            def _(u):
                for k in range(UNROLL):
                    e = g * CHUNK + u * UNROLL + k
                    col = cols[e]
                    col = ((col // 2 - row_id // 2) & 3) * 2 + ((col ^ row_id) & 1)
                    col = jnp.where(e < count, col, COLBLK)
                    row = rows[e]
                    part = pl.ds(pl.multiple_of(row // 2 * RUN, RUN), RUN)
                    block = held[e].astype(F32).reshape(HALF, 2, RUN, BLOCK)
                    place = (col, row & 1, slice(None), slice(None), part, slice(None))
                    total[place] = total[place] + block

    out = []
    for p in range(2):
        for i in range(2):
            target, source = abs(1 - p - core), abs(1 - i - core)
            k = 2 * p + i
            for j in range(COLBLK):
                terms = total[j, source, :, target]
                done[k, :, j * BLOCK : (j + 1) * BLOCK] = (
                    terms.reshape(QUARTER, BLOCK).astype(done.dtype)
                )
            out.append(pltpu.make_async_copy(done.at[k], tile_ref.at[k], tile_sems.at[k]))
            out[-1].start()
    for copied in out:
        copied.wait()


def merge(tile_rows, tile_cols, stored, tile_blocks):
    quarter = (QUARTER, COLBLK * BLOCK)
    return pl.pallas_call(
        merge_kernel,
        out_shape=jax.ShapeDtypeStruct((ROOM,) + quarter, BF16),
        in_specs=[HBM] * 4,
        out_specs=HBM,
        scratch_shapes=[
            pltpu.SMEM((MAXB,), jnp.int32),
            pltpu.SMEM((MAXB,), jnp.int32),
            pltpu.SMEM((1,), jnp.int32),
            pltpu.VMEM((MAXB, BLOCK, BLOCK), BF16),
            pltpu.VMEM((COLBLK + 1, 2, HALF, 2, HALF * RUN, BLOCK), F32),
            pltpu.VMEM((4,) + quarter, BF16),
            pltpu.SemaphoreType.DMA((3,)),
            pltpu.SemaphoreType.DMA((MAXB // CHUNK,)),
            pltpu.SemaphoreType.DMA((4,)),
        ],
        compiler_params=pltpu.CompilerParams(vmem_limit_bytes=MERGE_VMEM),
        cost_estimate=pl.CostEstimate(
            flops=MAXB * BLOCK * BLOCK,
            bytes_accessed=(MAXB + BR * COLBLK) * BLOCK * BLOCK * 2,
            transcendentals=0,
        ),
        name="merge_blocks",
    )(tile_rows, tile_cols, stored, tile_blocks)


def copies_kernel(own_ref, out_ref, held, own_sem, sems):
    load = pltpu.make_async_copy(own_ref, held, own_sem)
    load.start()
    load.wait()
    stores = [
        pltpu.make_async_copy(held, out_ref.at[k], sems.at[k]) for k in range(out_ref.shape[0])
    ]
    for store in stores:
        store.start()
    for store in stores:
        store.wait()


def copies(own, count):
    return pl.pallas_call(
        copies_kernel,
        out_shape=jax.ShapeDtypeStruct((count,) + own.shape, own.dtype),
        in_specs=[HBM],
        out_specs=HBM,
        scratch_shapes=[
            pltpu.VMEM(own.shape, own.dtype),
            pltpu.SemaphoreType.DMA,
            pltpu.SemaphoreType.DMA((count,)),
        ],
        compiler_params=pltpu.CompilerParams(vmem_limit_bytes=MERGE_VMEM),
        name="copies",
    )(own)


def dot(a, b):
    return jnp.dot(a, b, preferred_element_type=F32)


def put_together(part_refs, panel):
    rows = panel.shape[0] // len(part_refs)
    for k, part_ref in enumerate(part_refs):
        panel[k * rows : (k + 1) * rows, :] = part_ref[...]


def fetch_kernel(halves, tile_ref, *refs):
    *out_refs, sems = refs[-1 - len(halves) :]
    rows = QUARTER // PIECES
    copies = []
    for h, (out_ref, half) in enumerate(zip(out_refs, halves)):
        for q, quarter in enumerate(half):
            for k in range(PIECES):
                part = pl.ds(k * rows, rows)
                copies.append(
                    pltpu.make_async_copy(
                        tile_ref.at[quarter, part], out_ref.at[q, part], sems.at[h, q, k]
                    )
                )
                copies[-1].start()
    for copy in copies:
        copy.wait()


def step_kernel(first, keep, *refs):
    tile_ref, refs = refs[0], refs[1:]
    refs, (panel, total) = refs[:-2], refs[-2:]
    row_id, col_id = lax.axis_index("row"), lax.axis_index("col")
    core = col_id & 1
    if first:
        dealt_ref, out_ref = refs[:2]
        for k in range(COLBLK):
            part = ((row_id // 2 + k // 2) & 3) * 2 + ((row_id ^ k) & 1)
            part = pl.ds(pl.multiple_of(part * BLOCK, BLOCK), BLOCK)
            panel[k * BLOCK : (k + 1) * BLOCK, :] = dealt_ref[part, :]
        if not keep:
            refs[2][...] = panel[:PAIR, :]
    else:
        out_ref = refs[4]
        put_together([refs[k] for k in PANEL_ORDER], panel)
    for i in range(2):
        terms = dot(tile_ref[i], panel[...])
        terms = terms.reshape(HALF, HALF, RUN, terms.shape[1])
        for t in range(HALF):
            away = ((t // 2 - col_id // 4) & 3) * 2 + ((t ^ (col_id // 2)) & 1)
            total[away, :, core if i else 1 - core] = terms[t]
    out_ref[...] = total[...].reshape(out_ref.shape).astype(out_ref.dtype)


def last_kernel(keep, tile_ref, *refs):
    parts, (first_ref, out_ref, panel, total) = refs[:4], refs[4:]
    put_together([parts[k] for k in PANEL_ORDER], panel)
    col_id = lax.axis_index("col")
    core = col_id & 1
    for j in range(2):
        terms = dot(tile_ref[j], panel[...])
        terms = terms.reshape(HALF, HALF, RUN, terms.shape[1])
        for t in range(HALF):
            total[:, t, core if j else 1 - core] = terms[t]
    first = first_ref[:BLOCK, :].astype(F32).reshape(HALF, 2, RUN, first_ref.shape[1])
    target = core if keep else 1 - core
    first = jnp.where(target == 0, first[:, 0], first[:, 1])
    mine = col_id // 2
    total[:, mine, core] = total[:, mine, core] - 0.5 * first
    out_ref[...] = total[...].reshape(out_ref.shape).astype(out_ref.dtype)


def add_kernel(a_ref, b_ref, *out_refs):
    rows = out_refs[0].shape[0]
    for k, out_ref in enumerate(out_refs):
        part = slice(k * rows, (k + 1) * rows)
        out_ref[...] = (a_ref[part, :].astype(F32) + b_ref[part, :].astype(F32)).astype(BF16)


def sum_kernel(a_ref, b_ref, c_ref, d_ref, *out_refs):
    rows = out_refs[0].shape[0]
    for k, out_ref in enumerate(out_refs):
        part = slice(k * rows, (k + 1) * rows)
        terms = [ref[part, :].astype(F32) for ref in (a_ref, b_ref, c_ref, d_ref)]
        out_ref[...] = ((terms[0] + terms[1]) + (terms[2] + terms[3])).astype(BF16)


def next_kernel(scale, own_ref, arrived_ref, far_ref, near_ref, *refs):
    out_ref = refs[-1]
    pairs = ((own_ref, arrived_ref), (near_ref, far_ref))
    for k, (a_ref, b_ref) in enumerate(pairs):
        part = slice(k * BLOCK, (k + 1) * BLOCK)
        summed = a_ref[...].astype(F32) + b_ref[...].astype(F32)
        if len(refs) > 1:
            summed = scale * summed - refs[0][part, :].astype(F32)
        out_ref[part, :] = summed.astype(BF16)


def per_device(vectors, blocks, block_rows, block_cols, counts):
    col_count = lax.axis_size("col")
    row_count = lax.axis_size("row")
    devices = row_count * col_count
    shard_rows, width = vectors.shape
    half_rows = 2 * QUARTER
    flops = 2 * half_rows * COLBLK * BLOCK * width

    def exchange(parts, axes, groups=None):
        return lax.all_to_all(
            parts, axes, split_axis=0, concat_axis=0, tiled=True, axis_index_groups=groups
        )

    def other_core(x):
        return lax.ppermute(x, "col", [(i, i ^ 1) for i in range(col_count)])

    def along_x(x, k):
        return lax.ppermute(x, "col", [(i, (i + 4 * k) % col_count) for i in range(col_count)])

    def along_y(x, k):
        return lax.ppermute(x, "row", [(i, (i + 2 * k) % row_count) for i in range(row_count)])

    def near_z(x):
        return lax.ppermute(x, "row", [(i, i ^ 1) for i in range(row_count)])

    def far_z(x):
        return lax.ppermute(x, "col", [(i, i ^ 2) for i in range(col_count)])

    def both_z(x):
        pairs = [
            (r * col_count + c, (r ^ 1) * col_count + (c ^ 2))
            for r in range(row_count)
            for c in range(col_count)
        ]
        return lax.ppermute(x, ("row", "col"), pairs)

    scratch = [
        pltpu.VMEM((COLBLK * BLOCK, width), BF16),
        pltpu.VMEM((HALF, HALF, 2, RUN, width), F32),
    ]
    sems = pltpu.SemaphoreType.DMA((2, 2, PIECES))
    quarters = (2, QUARTER, COLBLK * BLOCK)

    def fetch(tile, *halves, after=()):
        kernel = functools.partial(fetch_kernel, halves)
        return small_call(kernel, "fetch", [quarters] * len(halves), after, [sems], 0, tile)

    def product(kernel, name, fetched, operands, more=()):
        wide = (half_rows, width)
        sent, *rest = small_call(
            functools.partial(kernel, False),
            name + "_send",
            [wide, *more],
            (fetched[0], *operands),
            scratch,
            flops,
        )
        arrived = other_core(sent)
        (kept,) = small_call(
            functools.partial(kernel, True),
            name + "_keep",
            [wide],
            (fetched[1], *operands),
            scratch,
            flops,
        )
        return (kept, arrived), rest

    def step(tile, fetched, parts, first, previous, which):
        kernel = functools.partial(step_kernel, first)
        more = [(PAIR, width)] if first else []
        terms, rest = product(kernel, "first" if first else "step", fetched, parts, more)
        terms = small_call(add_kernel, "add", [(PAIR, width)] * 4, terms)
        arrived = [along_x(terms[k], k) for k in (2, 1, 3)]
        fetched = fetch(tile, *which, after=(terms[0],))
        own, other = small_call(
            sum_kernel, "sum_x", [(BLOCK, width)] * 2, (terms[0], *arrived)
        )
        near, far, arrived = near_z(own), both_z(other), far_z(other)
        operands = (own, arrived, far, near) + (() if first else (previous,))
        (pair,) = small_call(
            functools.partial(next_kernel, 2.0), "next", [(PAIR, width)], operands
        )
        sides = {k: along_y(pair, k) for k in (1, 3, 2)}
        return (pair, sides[1], sides[3], sides[2]), fetched, (rest[0] if first else None)

    with jax.named_scope("merge"):
        tile = merge(block_rows[0, 0], block_cols[0, 0], counts[0], blocks[0, 0])
    with jax.named_scope("deal"):
        panel = exchange(copies(vectors, row_count).reshape(devices, RUN, width), ("row", "col"))
        panel = panel.reshape(row_count * shard_rows, width)
    with jax.named_scope("step1"):
        fetched = [*fetch(tile, (0, 1)), *fetch(tile, (2, 3))]
        parts, fetched, previous = step(tile, fetched, (panel,), True, None, ((0, 1), (2, 3)))
        first = parts[0]
    with jax.named_scope("step2"):
        parts, fetched, _ = step(tile, fetched, parts, False, previous, ((0, 2), (1, 3)))
    with jax.named_scope("step3"):
        terms, _ = product(last_kernel, "last", fetched, parts + (first,))
        (terms,) = small_call(add_kernel, "add", [(half_rows, width)], terms)
        same_core = [list(range(c, col_count, 2)) for c in range(2)]
        arrived = exchange(terms.reshape(HALF, shard_rows, width), "col", same_core)
        summed = jnp.sum(arrived.astype(F32), axis=0)
        filtered = (2.0 * summed).astype(BF16)
    with jax.named_scope("gram"):
        local = (dot(filtered.T, filtered) / (BR * BLOCK // col_count)).astype(BF16)
        arrived = exchange(local.reshape(devices, width // devices, width), ("row", "col"))
        gram = jnp.sum(arrived.astype(F32), axis=0)
    return filtered, gram


def solution(mesh):
    in_specs = (
        P(("row", "col"), None),
        P("row", "col", None, None, None),
        P("row", "col", None),
        P("row", "col", None),
        P("row", "col"),
    )
    out_specs = (P(("row", "col"), None), P(("row", "col"), None))
    return jax.shard_map(
        per_device, mesh=mesh, in_specs=in_specs, out_specs=out_specs, check_vma=False
    )
```

```python
import functools

import jax
import jax.numpy as jnp
from jax import lax
from jax.experimental import pallas as pl
from jax.experimental.pallas import tpu as pltpu
from jax.sharding import PartitionSpec as P

BLOCK = 128
BR = 16
COLBLK = 8
MAXB = 256
RUN = 8
HALF = 8
QUARTER = HALF * HALF * RUN
PAIR = 2 * BLOCK
CHUNK = 16
UNROLL = 16
PANEL_ORDER = (0, 2, 3, 1)
PIECES = 2
MERGE_VMEM = 60 * 1024 * 1024
SMALL_VMEM = 8 * 1024 * 1024
PRODUCT_VMEM = 50 * 1024 * 1024
ROOM = 16
VMEM = pl.BlockSpec(memory_space=pltpu.VMEM)
HBM = pl.BlockSpec(memory_space=pltpu.HBM)
F32 = jnp.float32
BF16 = jnp.bfloat16


def small_call(kernel, name, out_shapes, operands, scratch=(), flops=0, tile=None):
    tiles = [] if tile is None else [tile]
    outs = [jax.ShapeDtypeStruct(shape, BF16) for shape in out_shapes]
    sizes = sum(x.size for x in operands) + sum(x.size for x in outs)
    return pl.pallas_call(
        kernel,
        out_shape=outs,
        in_specs=[HBM] * len(tiles) + [VMEM] * len(operands),
        out_specs=[VMEM] * len(outs),
        scratch_shapes=list(scratch),
        compiler_params=pltpu.CompilerParams(vmem_limit_bytes=PRODUCT_VMEM if tiles else SMALL_VMEM),
        cost_estimate=pl.CostEstimate(
            flops=flops, bytes_accessed=2 * sizes, transcendentals=0
        ),
        name=name,
    )(*tiles, *operands)


def merge_kernel(
    rows_ref, cols_ref, stored_ref, blocks_ref, tile_ref,
    rows, cols, stored, held, total, done, index_sems, sems, tile_sems,
):
    row_id, core = lax.axis_index("row"), lax.axis_index("col") & 1
    chunks = MAXB // CHUNK
    indices = [
        pltpu.make_async_copy(source, target, index_sems.at[k])
        for k, (source, target) in enumerate(
            ((stored_ref, stored), (rows_ref, rows), (cols_ref, cols))
        )
    ]

    def copy(g):
        part = pl.ds(g * CHUNK, CHUNK)
        return pltpu.make_async_copy(blocks_ref.at[part], held.at[part], sems.at[g])

    for index in indices:
        index.start()
    for g in range(chunks):
        copy(g).start()

    @pl.loop(0, COLBLK)
    def _(j):
        total[j] = jnp.zeros(total.shape[1:], total.dtype)

    for index in indices:
        index.wait()
    count = stored[0]

    @pl.loop(0, chunks)
    def _(g):
        copy(g).wait()

        @pl.when(g * CHUNK < count)
        def _():
            @pl.loop(0, CHUNK // UNROLL)
            def _(u):
                for k in range(UNROLL):
                    e = g * CHUNK + u * UNROLL + k
                    col = cols[e]
                    col = ((col // 2 - row_id // 2) & 3) * 2 + ((col ^ row_id) & 1)
                    col = jnp.where(e < count, col, COLBLK)
                    row = rows[e]
                    part = pl.ds(pl.multiple_of(row // 2 * RUN, RUN), RUN)
                    block = held[e].astype(F32).reshape(HALF, 2, RUN, BLOCK)
                    place = (col, row & 1, slice(None), slice(None), part, slice(None))
                    total[place] = total[place] + block

    out = []
    for p in range(2):
        for i in range(2):
            target, source = abs(1 - p - core), abs(1 - i - core)
            k = 2 * p + i
            for j in range(COLBLK):
                terms = total[j, source, :, target]
                done[k, :, j * BLOCK : (j + 1) * BLOCK] = (
                    terms.reshape(QUARTER, BLOCK).astype(done.dtype)
                )
            out.append(pltpu.make_async_copy(done.at[k], tile_ref.at[k], tile_sems.at[k]))
            out[-1].start()
    for copied in out:
        copied.wait()


def merge(tile_rows, tile_cols, stored, tile_blocks):
    quarter = (QUARTER, COLBLK * BLOCK)
    return pl.pallas_call(
        merge_kernel,
        out_shape=jax.ShapeDtypeStruct((ROOM,) + quarter, BF16),
        in_specs=[HBM] * 4,
        out_specs=HBM,
        scratch_shapes=[
            pltpu.SMEM((MAXB,), jnp.int32),
            pltpu.SMEM((MAXB,), jnp.int32),
            pltpu.SMEM((1,), jnp.int32),
            pltpu.VMEM((MAXB, BLOCK, BLOCK), BF16),
            pltpu.VMEM((COLBLK + 1, 2, HALF, 2, HALF * RUN, BLOCK), F32),
            pltpu.VMEM((4,) + quarter, BF16),
            pltpu.SemaphoreType.DMA((3,)),
            pltpu.SemaphoreType.DMA((MAXB // CHUNK,)),
            pltpu.SemaphoreType.DMA((4,)),
        ],
        compiler_params=pltpu.CompilerParams(vmem_limit_bytes=MERGE_VMEM),
        cost_estimate=pl.CostEstimate(
            flops=MAXB * BLOCK * BLOCK,
            bytes_accessed=(MAXB + BR * COLBLK) * BLOCK * BLOCK * 2,
            transcendentals=0,
        ),
        name="merge_blocks",
    )(tile_rows, tile_cols, stored, tile_blocks)


def copies_kernel(own_ref, out_ref, held, own_sem, sems):
    load = pltpu.make_async_copy(own_ref, held, own_sem)
    load.start()
    load.wait()
    stores = [
        pltpu.make_async_copy(held, out_ref.at[k], sems.at[k]) for k in range(out_ref.shape[0])
    ]
    for store in stores:
        store.start()
    for store in stores:
        store.wait()


def copies(own, count):
    return pl.pallas_call(
        copies_kernel,
        out_shape=jax.ShapeDtypeStruct((count,) + own.shape, own.dtype),
        in_specs=[HBM],
        out_specs=HBM,
        scratch_shapes=[
            pltpu.VMEM(own.shape, own.dtype),
            pltpu.SemaphoreType.DMA,
            pltpu.SemaphoreType.DMA((count,)),
        ],
        compiler_params=pltpu.CompilerParams(vmem_limit_bytes=MERGE_VMEM),
        name="copies",
    )(own)


def dot(a, b):
    return jnp.dot(a, b, preferred_element_type=F32)


def put_together(part_refs, panel):
    rows = panel.shape[0] // len(part_refs)
    for k, part_ref in enumerate(part_refs):
        panel[k * rows : (k + 1) * rows, :] = part_ref[...]


def fetch_kernel(halves, tile_ref, *refs):
    *out_refs, sems = refs[-1 - len(halves) :]
    rows = QUARTER // PIECES
    copies = []
    for h, (out_ref, half) in enumerate(zip(out_refs, halves)):
        for q, quarter in enumerate(half):
            for k in range(PIECES):
                part = pl.ds(k * rows, rows)
                copies.append(
                    pltpu.make_async_copy(
                        tile_ref.at[quarter, part], out_ref.at[q, part], sems.at[h, q, k]
                    )
                )
                copies[-1].start()
    for copy in copies:
        copy.wait()


def step_kernel(first, keep, *refs):
    tile_ref, refs = refs[0], refs[1:]
    refs, (panel, total) = refs[:-2], refs[-2:]
    row_id, col_id = lax.axis_index("row"), lax.axis_index("col")
    core = col_id & 1
    if first:
        dealt_ref, out_ref = refs[:2]
        for k in range(COLBLK):
            part = ((row_id // 2 + k // 2) & 3) * 2 + ((row_id ^ k) & 1)
            part = pl.ds(pl.multiple_of(part * BLOCK, BLOCK), BLOCK)
            panel[k * BLOCK : (k + 1) * BLOCK, :] = dealt_ref[part, :]
        if not keep:
            refs[2][...] = panel[:PAIR, :]
    else:
        out_ref = refs[4]
        put_together([refs[k] for k in PANEL_ORDER], panel)
    both = dot(tile_ref[...].reshape(2 * QUARTER, panel.shape[0]), panel[...])
    both = both.reshape(2, HALF, HALF, RUN, panel.shape[1])
    for i in range(2):
        terms = both[i]
        for t in range(HALF):
            away = ((t // 2 - col_id // 4) & 3) * 2 + ((t ^ (col_id // 2)) & 1)
            total[away, :, core if i else 1 - core] = terms[t]
    out_ref[...] = total[...].reshape(out_ref.shape).astype(out_ref.dtype)


def last_kernel(keep, tile_ref, *refs):
    parts, (first_ref, out_ref, panel, total) = refs[:4], refs[4:]
    put_together([parts[k] for k in PANEL_ORDER], panel)
    col_id = lax.axis_index("col")
    core = col_id & 1
    both = dot(tile_ref[...].reshape(2 * QUARTER, panel.shape[0]), panel[...])
    both = both.reshape(2, HALF, HALF, RUN, panel.shape[1])
    for j in range(2):
        terms = both[j]
        for t in range(HALF):
            total[:, t, core if j else 1 - core] = terms[t]
    first = first_ref[:BLOCK, :].astype(F32).reshape(HALF, 2, RUN, first_ref.shape[1])
    target = core if keep else 1 - core
    first = jnp.where(target == 0, first[:, 0], first[:, 1])
    mine = col_id // 2
    total[:, mine, core] = total[:, mine, core] - 0.5 * first
    out_ref[...] = total[...].reshape(out_ref.shape).astype(out_ref.dtype)


def add_kernel(a_ref, b_ref, *out_refs):
    rows = out_refs[0].shape[0]
    for k, out_ref in enumerate(out_refs):
        part = slice(k * rows, (k + 1) * rows)
        out_ref[...] = (a_ref[part, :].astype(F32) + b_ref[part, :].astype(F32)).astype(BF16)


def sum_kernel(a_ref, b_ref, c_ref, d_ref, *out_refs):
    rows = out_refs[0].shape[0]
    for k, out_ref in enumerate(out_refs):
        part = slice(k * rows, (k + 1) * rows)
        terms = [ref[part, :].astype(F32) for ref in (a_ref, b_ref, c_ref, d_ref)]
        out_ref[...] = ((terms[0] + terms[1]) + (terms[2] + terms[3])).astype(BF16)


def next_kernel(scale, own_ref, arrived_ref, far_ref, near_ref, *refs):
    out_ref = refs[-1]
    pairs = ((own_ref, arrived_ref), (near_ref, far_ref))
    for k, (a_ref, b_ref) in enumerate(pairs):
        part = slice(k * BLOCK, (k + 1) * BLOCK)
        summed = a_ref[...].astype(F32) + b_ref[...].astype(F32)
        if len(refs) > 1:
            summed = scale * summed - refs[0][part, :].astype(F32)
        out_ref[part, :] = summed.astype(BF16)


def per_device(vectors, blocks, block_rows, block_cols, counts):
    col_count = lax.axis_size("col")
    row_count = lax.axis_size("row")
    devices = row_count * col_count
    shard_rows, width = vectors.shape
    half_rows = 2 * QUARTER
    flops = 2 * half_rows * COLBLK * BLOCK * width

    def exchange(parts, axes, groups=None):
        return lax.all_to_all(
            parts, axes, split_axis=0, concat_axis=0, tiled=True, axis_index_groups=groups
        )

    def other_core(x):
        return lax.ppermute(x, "col", [(i, i ^ 1) for i in range(col_count)])

    def along_x(x, k):
        return lax.ppermute(x, "col", [(i, (i + 4 * k) % col_count) for i in range(col_count)])

    def along_y(x, k):
        return lax.ppermute(x, "row", [(i, (i + 2 * k) % row_count) for i in range(row_count)])

    def near_z(x):
        return lax.ppermute(x, "row", [(i, i ^ 1) for i in range(row_count)])

    def far_z(x):
        return lax.ppermute(x, "col", [(i, i ^ 2) for i in range(col_count)])

    def both_z(x):
        pairs = [
            (r * col_count + c, (r ^ 1) * col_count + (c ^ 2))
            for r in range(row_count)
            for c in range(col_count)
        ]
        return lax.ppermute(x, ("row", "col"), pairs)

    scratch = [
        pltpu.VMEM((COLBLK * BLOCK, width), BF16),
        pltpu.VMEM((HALF, HALF, 2, RUN, width), F32),
    ]
    sems = pltpu.SemaphoreType.DMA((2, 2, PIECES))
    quarters = (2, QUARTER, COLBLK * BLOCK)

    def fetch(tile, *halves, after=()):
        kernel = functools.partial(fetch_kernel, halves)
        return small_call(kernel, "fetch", [quarters] * len(halves), after, [sems], 0, tile)

    def product(kernel, name, fetched, operands, more=()):
        wide = (half_rows, width)
        sent, *rest = small_call(
            functools.partial(kernel, False),
            name + "_send",
            [wide, *more],
            (fetched[0], *operands),
            scratch,
            flops,
        )
        arrived = other_core(sent)
        (kept,) = small_call(
            functools.partial(kernel, True),
            name + "_keep",
            [wide],
            (fetched[1], *operands),
            scratch,
            flops,
        )
        return (kept, arrived), rest

    def step(tile, fetched, parts, first, previous, which):
        kernel = functools.partial(step_kernel, first)
        more = [(PAIR, width)] if first else []
        terms, rest = product(kernel, "first" if first else "step", fetched, parts, more)
        terms = small_call(add_kernel, "add", [(PAIR, width)] * 4, terms)
        arrived = [along_x(terms[k], k) for k in (2, 1, 3)]
        fetched = fetch(tile, *which, after=(terms[0],))
        own, other = small_call(
            sum_kernel, "sum_x", [(BLOCK, width)] * 2, (terms[0], *arrived)
        )
        near, far, arrived = near_z(own), both_z(other), far_z(other)
        operands = (own, arrived, far, near) + (() if first else (previous,))
        (pair,) = small_call(
            functools.partial(next_kernel, 2.0), "next", [(PAIR, width)], operands
        )
        sides = {k: along_y(pair, k) for k in (1, 3, 2)}
        return (pair, sides[1], sides[3], sides[2]), fetched, (rest[0] if first else None)

    with jax.named_scope("merge"):
        tile = merge(block_rows[0, 0], block_cols[0, 0], counts[0], blocks[0, 0])
    with jax.named_scope("deal"):
        panel = exchange(copies(vectors, row_count).reshape(devices, RUN, width), ("row", "col"))
        panel = panel.reshape(row_count * shard_rows, width)
    with jax.named_scope("step1"):
        fetched = [*fetch(tile, (0, 1)), *fetch(tile, (2, 3))]
        parts, fetched, previous = step(tile, fetched, (panel,), True, None, ((0, 1), (2, 3)))
        first = parts[0]
    with jax.named_scope("step2"):
        parts, fetched, _ = step(tile, fetched, parts, False, previous, ((0, 2), (1, 3)))
    with jax.named_scope("step3"):
        terms, _ = product(last_kernel, "last", fetched, parts + (first,))
        (terms,) = small_call(add_kernel, "add", [(half_rows, width)], terms)
        same_core = [list(range(c, col_count, 2)) for c in range(2)]
        arrived = exchange(terms.reshape(HALF, shard_rows, width), "col", same_core)
        summed = jnp.sum(arrived.astype(F32), axis=0)
        filtered = (2.0 * summed).astype(BF16)
    with jax.named_scope("gram"):
        local = (dot(filtered.T, filtered) / (BR * BLOCK // col_count)).astype(BF16)
        arrived = exchange(local.reshape(devices, width // devices, width), ("row", "col"))
        gram = jnp.sum(arrived.astype(F32), axis=0)
    return filtered, gram


def solution(mesh):
    in_specs = (
        P(("row", "col"), None),
        P("row", "col", None, None, None),
        P("row", "col", None),
        P("row", "col", None),
        P("row", "col"),
    )
    out_specs = (P(("row", "col"), None), P(("row", "col"), None))
    return jax.shard_map(
        per_device, mesh=mesh, in_specs=in_specs, out_specs=out_specs, check_vma=False
    )
```

```python
import functools

import jax
import jax.numpy as jnp
from jax import lax
from jax.experimental import pallas as pl
from jax.experimental.pallas import tpu as pltpu
from jax.sharding import PartitionSpec as P

BLOCK = 128
BR = 16
COLBLK = 8
MAXB = 256
RUN = 8
HALF = 8
QUARTER = HALF * HALF * RUN
PAIR = 2 * BLOCK
CHUNK = 16
UNROLL = 16
PANEL_ORDER = (0, 2, 3, 1)
PIECES = 2
MERGE_VMEM = 60 * 1024 * 1024
SMALL_VMEM = 8 * 1024 * 1024
PRODUCT_VMEM = 50 * 1024 * 1024
ROOM = 16
VMEM = pl.BlockSpec(memory_space=pltpu.VMEM)
HBM = pl.BlockSpec(memory_space=pltpu.HBM)
F32 = jnp.float32
BF16 = jnp.bfloat16


def small_call(kernel, name, out_shapes, operands, scratch=(), flops=0, tile=None, far=False):
    tiles = [] if tile is None else [tile]
    outs = [jax.ShapeDtypeStruct(shape, BF16) for shape in out_shapes]
    sizes = sum(x.size for x in operands) + sum(x.size for x in outs)
    return pl.pallas_call(
        kernel,
        out_shape=outs,
        in_specs=[HBM] * len(tiles) + [VMEM] * len(operands),
        out_specs=[VMEM] + [HBM if far else VMEM] * (len(outs) - 1),
        scratch_shapes=list(scratch),
        compiler_params=pltpu.CompilerParams(vmem_limit_bytes=PRODUCT_VMEM if tiles else SMALL_VMEM),
        cost_estimate=pl.CostEstimate(
            flops=flops, bytes_accessed=2 * sizes, transcendentals=0
        ),
        name=name,
    )(*tiles, *operands)


def merge_kernel(
    rows_ref, cols_ref, stored_ref, blocks_ref, tile_ref,
    rows, cols, stored, held, total, done, index_sems, sems, tile_sems,
):
    row_id, core = lax.axis_index("row"), lax.axis_index("col") & 1
    chunks = MAXB // CHUNK
    indices = [
        pltpu.make_async_copy(source, target, index_sems.at[k])
        for k, (source, target) in enumerate(
            ((stored_ref, stored), (rows_ref, rows), (cols_ref, cols))
        )
    ]

    def copy(g):
        part = pl.ds(g * CHUNK, CHUNK)
        return pltpu.make_async_copy(blocks_ref.at[part], held.at[part], sems.at[g])

    for index in indices:
        index.start()
    for g in range(chunks):
        copy(g).start()

    @pl.loop(0, COLBLK)
    def _(j):
        total[j] = jnp.zeros(total.shape[1:], total.dtype)

    for index in indices:
        index.wait()
    count = stored[0]

    @pl.loop(0, chunks)
    def _(g):
        copy(g).wait()

        @pl.when(g * CHUNK < count)
        def _():
            @pl.loop(0, CHUNK // UNROLL)
            def _(u):
                for k in range(UNROLL):
                    e = g * CHUNK + u * UNROLL + k
                    col = cols[e]
                    col = ((col // 2 - row_id // 2) & 3) * 2 + ((col ^ row_id) & 1)
                    col = jnp.where(e < count, col, COLBLK)
                    row = rows[e]
                    part = pl.ds(pl.multiple_of(row // 2 * RUN, RUN), RUN)
                    block = held[e].astype(F32).reshape(HALF, 2, RUN, BLOCK)
                    place = (col, row & 1, slice(None), slice(None), part, slice(None))
                    total[place] = total[place] + block

    out = []
    for p in range(2):
        for i in range(2):
            target, source = abs(1 - p - core), abs(1 - i - core)
            k = 2 * p + i
            for j in range(COLBLK):
                terms = total[j, source, :, target]
                done[k, :, j * BLOCK : (j + 1) * BLOCK] = (
                    terms.reshape(QUARTER, BLOCK).astype(done.dtype)
                )
            out.append(pltpu.make_async_copy(done.at[k], tile_ref.at[k], tile_sems.at[k]))
            out[-1].start()
    for copied in out:
        copied.wait()


def merge(tile_rows, tile_cols, stored, tile_blocks):
    quarter = (QUARTER, COLBLK * BLOCK)
    return pl.pallas_call(
        merge_kernel,
        out_shape=jax.ShapeDtypeStruct((ROOM,) + quarter, BF16),
        in_specs=[HBM] * 4,
        out_specs=HBM,
        scratch_shapes=[
            pltpu.SMEM((MAXB,), jnp.int32),
            pltpu.SMEM((MAXB,), jnp.int32),
            pltpu.SMEM((1,), jnp.int32),
            pltpu.VMEM((MAXB, BLOCK, BLOCK), BF16),
            pltpu.VMEM((COLBLK + 1, 2, HALF, 2, HALF * RUN, BLOCK), F32),
            pltpu.VMEM((4,) + quarter, BF16),
            pltpu.SemaphoreType.DMA((3,)),
            pltpu.SemaphoreType.DMA((MAXB // CHUNK,)),
            pltpu.SemaphoreType.DMA((4,)),
        ],
        compiler_params=pltpu.CompilerParams(vmem_limit_bytes=MERGE_VMEM),
        cost_estimate=pl.CostEstimate(
            flops=MAXB * BLOCK * BLOCK,
            bytes_accessed=(MAXB + BR * COLBLK) * BLOCK * BLOCK * 2,
            transcendentals=0,
        ),
        name="merge_blocks",
    )(tile_rows, tile_cols, stored, tile_blocks)


def copies_kernel(own_ref, out_ref, held, own_sem, sems):
    load = pltpu.make_async_copy(own_ref, held, own_sem)
    load.start()
    load.wait()
    stores = [
        pltpu.make_async_copy(held, out_ref.at[k], sems.at[k]) for k in range(out_ref.shape[0])
    ]
    for store in stores:
        store.start()
    for store in stores:
        store.wait()


def copies(own, count):
    return pl.pallas_call(
        copies_kernel,
        out_shape=jax.ShapeDtypeStruct((count,) + own.shape, own.dtype),
        in_specs=[HBM],
        out_specs=HBM,
        scratch_shapes=[
            pltpu.VMEM(own.shape, own.dtype),
            pltpu.SemaphoreType.DMA,
            pltpu.SemaphoreType.DMA((count,)),
        ],
        compiler_params=pltpu.CompilerParams(vmem_limit_bytes=MERGE_VMEM),
        name="copies",
    )(own)


def dot(a, b):
    return jnp.dot(a, b, preferred_element_type=F32)


def put_together(part_refs, panel):
    rows = panel.shape[0] // len(part_refs)
    for k, part_ref in enumerate(part_refs):
        panel[k * rows : (k + 1) * rows, :] = part_ref[...]


def fetch_kernel(halves, tile_ref, *refs):
    *out_refs, held, sems, store_sems = refs[-3 - len(halves) :]
    rows = QUARTER // PIECES
    copies, stores = [], []
    for h, (out_ref, half) in enumerate(zip(out_refs, halves)):
        for q, quarter in enumerate(half):
            for k in range(PIECES):
                part = pl.ds(k * rows, rows)
                target = held.at[q, part] if h else out_ref.at[q, part]
                copies.append(
                    pltpu.make_async_copy(tile_ref.at[quarter, part], target, sems.at[h, q, k])
                )
                copies[-1].start()
                if h:
                    store = pltpu.make_async_copy(
                        target, out_ref.at[q, part], store_sems.at[q, k]
                    )
                    stores.append((len(copies) - 1, store))
    stored = dict(stores)
    for n, copy in enumerate(copies):
        copy.wait()
        if n in stored:
            stored[n].start()
    for _, store in stores:
        store.wait()


def step_kernel(first, keep, *refs):
    tile_ref, refs = refs[0], refs[1:]
    refs, (panel, total) = refs[:-2], refs[-2:]
    row_id, col_id = lax.axis_index("row"), lax.axis_index("col")
    core = col_id & 1
    if first:
        dealt_ref, out_ref = refs[:2]
        for k in range(COLBLK):
            part = ((row_id // 2 + k // 2) & 3) * 2 + ((row_id ^ k) & 1)
            part = pl.ds(pl.multiple_of(part * BLOCK, BLOCK), BLOCK)
            panel[k * BLOCK : (k + 1) * BLOCK, :] = dealt_ref[part, :]
        if not keep:
            refs[2][...] = panel[:PAIR, :]
    else:
        out_ref = refs[4]
        put_together([refs[k] for k in PANEL_ORDER], panel)
    both = dot(tile_ref[...].reshape(2 * QUARTER, panel.shape[0]), panel[...])
    both = both.reshape(2, HALF, HALF, RUN, panel.shape[1])
    for i in range(2):
        terms = both[i]
        for t in range(HALF):
            away = ((t // 2 - col_id // 4) & 3) * 2 + ((t ^ (col_id // 2)) & 1)
            total[away, :, core if i else 1 - core] = terms[t]
    out_ref[...] = total[...].reshape(out_ref.shape).astype(out_ref.dtype)


def last_kernel(keep, tile_ref, *refs):
    parts, (first_ref, out_ref, panel, total) = refs[:4], refs[4:]
    put_together([parts[k] for k in PANEL_ORDER], panel)
    col_id = lax.axis_index("col")
    core = col_id & 1
    both = dot(tile_ref[...].reshape(2 * QUARTER, panel.shape[0]), panel[...])
    both = both.reshape(2, HALF, HALF, RUN, panel.shape[1])
    for j in range(2):
        terms = both[j]
        for t in range(HALF):
            total[:, t, core if j else 1 - core] = terms[t]
    first = first_ref[:BLOCK, :].astype(F32).reshape(HALF, 2, RUN, first_ref.shape[1])
    target = core if keep else 1 - core
    first = jnp.where(target == 0, first[:, 0], first[:, 1])
    mine = col_id // 2
    total[:, mine, core] = total[:, mine, core] - 0.5 * first
    out_ref[...] = total[...].reshape(out_ref.shape).astype(out_ref.dtype)


def add_kernel(a_ref, b_ref, *out_refs):
    rows = out_refs[0].shape[0]
    for k, out_ref in enumerate(out_refs):
        part = slice(k * rows, (k + 1) * rows)
        out_ref[...] = (a_ref[part, :].astype(F32) + b_ref[part, :].astype(F32)).astype(BF16)


def sum_kernel(a_ref, b_ref, c_ref, d_ref, *out_refs):
    rows = out_refs[0].shape[0]
    for k, out_ref in enumerate(out_refs):
        part = slice(k * rows, (k + 1) * rows)
        terms = [ref[part, :].astype(F32) for ref in (a_ref, b_ref, c_ref, d_ref)]
        out_ref[...] = ((terms[0] + terms[1]) + (terms[2] + terms[3])).astype(BF16)


def next_kernel(scale, own_ref, arrived_ref, far_ref, near_ref, *refs):
    out_ref = refs[-1]
    pairs = ((own_ref, arrived_ref), (near_ref, far_ref))
    for k, (a_ref, b_ref) in enumerate(pairs):
        part = slice(k * BLOCK, (k + 1) * BLOCK)
        summed = a_ref[...].astype(F32) + b_ref[...].astype(F32)
        if len(refs) > 1:
            summed = scale * summed - refs[0][part, :].astype(F32)
        out_ref[part, :] = summed.astype(BF16)


def per_device(vectors, blocks, block_rows, block_cols, counts):
    col_count = lax.axis_size("col")
    row_count = lax.axis_size("row")
    devices = row_count * col_count
    shard_rows, width = vectors.shape
    half_rows = 2 * QUARTER
    flops = 2 * half_rows * COLBLK * BLOCK * width

    def exchange(parts, axes, groups=None):
        return lax.all_to_all(
            parts, axes, split_axis=0, concat_axis=0, tiled=True, axis_index_groups=groups
        )

    def other_core(x):
        return lax.ppermute(x, "col", [(i, i ^ 1) for i in range(col_count)])

    def along_x(x, k):
        return lax.ppermute(x, "col", [(i, (i + 4 * k) % col_count) for i in range(col_count)])

    def along_y(x, k):
        return lax.ppermute(x, "row", [(i, (i + 2 * k) % row_count) for i in range(row_count)])

    def near_z(x):
        return lax.ppermute(x, "row", [(i, i ^ 1) for i in range(row_count)])

    def far_z(x):
        return lax.ppermute(x, "col", [(i, i ^ 2) for i in range(col_count)])

    def both_z(x):
        pairs = [
            (r * col_count + c, (r ^ 1) * col_count + (c ^ 2))
            for r in range(row_count)
            for c in range(col_count)
        ]
        return lax.ppermute(x, ("row", "col"), pairs)

    scratch = [
        pltpu.VMEM((COLBLK * BLOCK, width), BF16),
        pltpu.VMEM((HALF, HALF, 2, RUN, width), F32),
    ]
    sems = pltpu.SemaphoreType.DMA((2, 2, PIECES))
    room = [pltpu.VMEM((2, QUARTER, COLBLK * BLOCK), BF16), sems]
    room.append(pltpu.SemaphoreType.DMA((2, PIECES)))
    quarters = (2, QUARTER, COLBLK * BLOCK)

    def fetch(tile, *halves, after=()):
        kernel = functools.partial(fetch_kernel, halves)
        return small_call(kernel, "fetch", [quarters] * len(halves), after, room, 0, tile, True)

    def product(kernel, name, fetched, operands, more=()):
        wide = (half_rows, width)
        sent, *rest = small_call(
            functools.partial(kernel, False),
            name + "_send",
            [wide, *more],
            (fetched[0], *operands),
            scratch,
            flops,
        )
        arrived = other_core(sent)
        (kept,) = small_call(
            functools.partial(kernel, True),
            name + "_keep",
            [wide],
            (fetched[1], *operands),
            scratch,
            flops,
        )
        return (kept, arrived), rest

    def step(tile, fetched, parts, first, previous, which):
        kernel = functools.partial(step_kernel, first)
        more = [(PAIR, width)] if first else []
        terms, rest = product(kernel, "first" if first else "step", fetched, parts, more)
        terms = small_call(add_kernel, "add", [(PAIR, width)] * 4, terms)
        arrived = [along_x(terms[k], k) for k in (2, 1, 3)]
        fetched = fetch(tile, *which, after=(terms[0],))
        own, other = small_call(
            sum_kernel, "sum_x", [(BLOCK, width)] * 2, (terms[0], *arrived)
        )
        near, far, arrived = near_z(own), both_z(other), far_z(other)
        operands = (own, arrived, far, near) + (() if first else (previous,))
        (pair,) = small_call(
            functools.partial(next_kernel, 2.0), "next", [(PAIR, width)], operands
        )
        sides = {k: along_y(pair, k) for k in (1, 3, 2)}
        return (pair, sides[1], sides[3], sides[2]), fetched, (rest[0] if first else None)

    with jax.named_scope("merge"):
        tile = merge(block_rows[0, 0], block_cols[0, 0], counts[0], blocks[0, 0])
    with jax.named_scope("deal"):
        panel = exchange(copies(vectors, row_count).reshape(devices, RUN, width), ("row", "col"))
        panel = panel.reshape(row_count * shard_rows, width)
    with jax.named_scope("step1"):
        fetched = [*fetch(tile, (0, 1)), *fetch(tile, (2, 3))]
        parts, fetched, previous = step(tile, fetched, (panel,), True, None, ((0, 1), (2, 3)))
        first = parts[0]
    with jax.named_scope("step2"):
        parts, fetched, _ = step(tile, fetched, parts, False, previous, ((0, 2), (1, 3)))
    with jax.named_scope("step3"):
        terms, _ = product(last_kernel, "last", fetched, parts + (first,))
        (terms,) = small_call(add_kernel, "add", [(half_rows, width)], terms)
        same_core = [list(range(c, col_count, 2)) for c in range(2)]
        arrived = exchange(terms.reshape(HALF, shard_rows, width), "col", same_core)
        summed = jnp.sum(arrived.astype(F32), axis=0)
        filtered = (2.0 * summed).astype(BF16)
    with jax.named_scope("gram"):
        local = (dot(filtered.T, filtered) / (BR * BLOCK // col_count)).astype(BF16)
        arrived = exchange(local.reshape(devices, width // devices, width), ("row", "col"))
        gram = jnp.sum(arrived.astype(F32), axis=0)
    return filtered, gram


def solution(mesh):
    in_specs = (
        P(("row", "col"), None),
        P("row", "col", None, None, None),
        P("row", "col", None),
        P("row", "col", None),
        P("row", "col"),
    )
    out_specs = (P(("row", "col"), None), P(("row", "col"), None))
    return jax.shard_map(
        per_device, mesh=mesh, in_specs=in_specs, out_specs=out_specs, check_vma=False
    )
```
